256 devices in a mesh: gx: 8 (over y, core), gz: 32 (over x, z).
Axes of the slice: x: 4, y: 4, z: 8, core: 2. Of those that a mesh axis runs over, the one named last changes fastest.
Arguments:
- velocity: float32 [3, 64, 256, 128], P(None, 'gx', 'gz'), may hold values from -6 to 6
- spacing: float32 [129], replicated, may hold values from 0.5 to 2
- basis: bfloat16 [128, 3, 64, 256, 128], P(None, None, 'gx', 'gz')
- history: bfloat16 [40, 3, 64, 256, 128], P(None, None, 'gx', 'gz')
- picks: int32 [31], replicated, may hold values from 0 to 39, as said below
Outputs:
- velocity_new: float32 [3, 64, 256, 128], P(None, 'gx', 'gz')
- factor: float32 [160, 160], replicated
- directions: bfloat16 [32, 3, 64, 256, 128], P(None, None, 'gx', 'gz')
The draws below stay inside these ranges and needn't reach their ends.
Inputs may be any that keep to these rules, and one draw needn't show every extreme that they name: `picks`: 31 distinct indices that always include 0 and 39.
All inputs are finite; a program needn't handle non-finite values.
Results may differ from the reference program's by a relative error of at most 0.0024.
The reference program's roundings to bfloat16 on the way count: a program that leaves them out, or rounds other values in their place, can miss the bound.
Values sent between devices are 32-bit elements; how exact they have to be, the bound alone decides.
No kernel may reach another device: no remote copies, remote signals or barrier semaphores. Data moves between devices by JAX's collectives and lax.ppermute only.
A program may use at most 192 MiB of HBM per device.

```python
import math
import jax
import jax.numpy as jnp
from jax import lax

NY = 128
RANK = 128
SNAPS = 32
HIST = 40
NX = 64
NZ = 256
ROWS = 6291456
COLS = 160


def cell_scale(key):
    key = jax.random.fold_in(key, 7)
    xs = jnp.arange(NX, dtype=jnp.float32)[:, None, None] / NX
    zs = jnp.arange(NZ, dtype=jnp.float32)[None, :, None] / NZ
    rough = jnp.exp(jax.random.uniform(key, (NX, NZ, NY), jnp.float32, -0.5, 0.5))
    return 10.0 ** ((xs + zs) * 0.5) / 3.0 * rough


def shared_modes(key):
    return jax.random.normal(jax.random.fold_in(key, 5), (HIST, 3, NX, NZ, NY), jnp.float32)


def draw_history(key, part):
    scale = cell_scale(key)
    common = shared_modes(key)
    key = jax.random.fold_in(key, 1)
    first, second = jax.random.split(key)
    noise = jax.random.normal(first, (HIST, 3, NX, NZ, NY), jnp.float32)
    amplitude = jnp.exp(jax.random.uniform(second, (HIST, 1, 1, 1, 1), jnp.float32, -0.7, 0.7))
    return ((common + 0.5 * noise) * amplitude * scale).astype(jnp.bfloat16)


def draw_basis(key, part):
    scale = cell_scale(key)
    common = shared_modes(key)
    key = jax.random.fold_in(key, 2)
    first, second = jax.random.split(key)
    noise = jax.random.normal(first, (RANK, 3, NX, NZ, NY), jnp.float32)
    amplitude = jnp.exp(jax.random.uniform(second, (RANK, 1, 1, 1, 1), jnp.float32, -1.2, 1.2))
    leading = 0.8 * common + 0.6 * noise[:HIST]
    modes = jnp.concatenate([leading, noise[HIST:]], axis=0)
    return (modes * amplitude * scale).astype(jnp.bfloat16)


def draw_picks(key, part):
    key = jax.random.fold_in(key, 3)
    first, second = jax.random.split(key)
    middle = 1 + jax.random.permutation(first, HIST - 2)[:SNAPS - 3]
    chosen = jnp.concatenate([jnp.array([0, HIST - 1], jnp.int32), middle.astype(jnp.int32)])
    return jax.random.permutation(second, chosen).astype(jnp.int32)


def level_of(rng, dims, shards, least, largest):
    factor_of = 1.0
    for position, parts in shards:
        steps = jax.random.uniform(jax.random.fold_in(jax.random.fold_in(rng, 6), position), (parts,), jnp.float32, least / len(shards), largest / len(shards))
        factor_of = factor_of * jnp.repeat(jnp.exp(steps), dims[position] // parts).reshape((-1,) + (1,) * (len(dims) - 1 - position))
    return factor_of


def centred(key, dims, scale, most, pieces=(), kind=jnp.bfloat16):
    entries = scale * jax.random.normal(key, dims, jnp.float32)
    if pieces:
        entries = entries * level_of(key, dims, pieces, -0.22, 0.18)
    return jnp.clip(entries, -most, most).astype(kind)


def setup_inputs(seed: int = 0) -> dict:
    keys = jax.random.split(jax.random.key(seed), 6)
    return {
        "velocity": centred(keys[0], (3, NX, NZ, NY), 1.0, 6.0, ((1, 8), (2, 32)), jnp.float32),
        "spacing": jnp.clip(jnp.exp(jax.random.uniform(keys[1], (NY + 1,), jnp.float32, math.log(0.5), math.log(2.0))), 0.5, 2.0),
        "basis": draw_basis(jax.random.fold_in(keys[5], 71), 0),
        "history": draw_history(jax.random.fold_in(keys[5], 71), 0),
        "picks": draw_picks(jax.random.fold_in(keys[5], 71), 0),
    }


step_size = 0.1
viscosity = 0.05
forcing = 0.5
gammas = (8.0 / 15.0, 5.0 / 12.0, 3.0 / 4.0)
zetas = (0.0, -17.0 / 60.0, -5.0 / 12.0)

def tendency(center, along_x, along_z, spacing):
    back_far, back_near, ahead_near, ahead_far = along_x
    side_far, side_near, front_near, front_far = along_z
    lower_gap = spacing[:-1]
    upper_gap = spacing[1:]
    padded_y = jnp.pad(center, ((0, 0), (0, 0), (0, 0), (1, 1)))
    beneath = padded_y[..., :-2]
    overhead = padded_y[..., 2:]
    grad_x = (8.0 * (ahead_near - back_near) - (ahead_far - back_far)) / 12.0
    grad_z = (8.0 * (front_near - side_near) - (front_far - side_far)) / 12.0
    grad_y = (overhead - beneath) / (lower_gap + upper_gap)
    curv_x = (-ahead_far + 16.0 * ahead_near - 30.0 * center + 16.0 * back_near - back_far) / 12.0
    curv_z = (-front_far + 16.0 * front_near - 30.0 * center + 16.0 * side_near - side_far) / 12.0
    curv_y = 2.0 * ((overhead - center) / upper_gap - (center - beneath) / lower_gap) / (lower_gap + upper_gap)
    advect = center[0:1] * grad_x + center[1:2] * grad_y + center[2:3] * grad_z
    push = jnp.array([forcing, 0.0, 0.0], jnp.float32)[:, None, None, None]
    return -advect + viscosity * (curv_x + curv_y + curv_z) + push

def reference(velocity, spacing, basis, history, picks):
    field = velocity
    previous = jnp.zeros_like(velocity)
    for section in range(3):
        along_x = tuple((jnp.roll(field, shift, axis=1) for shift in (2, 1, -1, -2)))
        along_z = tuple((jnp.roll(field, shift, axis=2) for shift in (2, 1, -1, -2)))
        current = tendency(field, along_x, along_z, spacing)
        field = field + step_size * (gammas[section] * current + zetas[section] * previous)
        previous = current
    fresh = field.astype(jnp.bfloat16)
    chosen = jnp.take(history, picks.astype(jnp.int32), axis=0)
    snapshots = jnp.concatenate([chosen, fresh[None]], axis=0)
    gram = jnp.zeros((COLS, COLS), jnp.float32)
    for comp in range(3):
        block = jnp.concatenate([basis[:, comp].reshape(RANK, -1), snapshots[:, comp].reshape(SNAPS, -1)], axis=0)
        gram = gram + lax.dot_general(block.astype(jnp.float32), block.astype(jnp.float32), (((1,), (1,)), ((), ())), preferred_element_type=jnp.float32)
    gram = gram / ROWS
    factor = jnp.linalg.cholesky(gram).T
    inverse = jax.scipy.linalg.solve_triangular(factor, jnp.eye(COLS, dtype=jnp.float32), lower=False)
    rounded = inverse.astype(jnp.bfloat16)
    directions = jnp.dot(rounded[:RANK, RANK:].T.astype(jnp.float32), basis.reshape(RANK, -1).astype(jnp.float32), preferred_element_type=jnp.float32)
    directions = directions + jnp.dot(rounded[RANK:, RANK:].T.astype(jnp.float32), snapshots.reshape(SNAPS, -1).astype(jnp.float32), preferred_element_type=jnp.float32)
    directions = directions.astype(jnp.bfloat16).reshape(SNAPS, 3, NX, NZ, NY)
    return (field, factor, directions)
```

```python
import jax
import jax.numpy as jnp
from jax import lax
from jax.experimental import pallas as pl
from jax.experimental.pallas import tpu as pltpu
from jax.sharding import PartitionSpec as P

step_size = 0.1
viscosity = 0.05
forcing = 0.5
gammas = (8.0 / 15.0, 5.0 / 12.0, 3.0 / 4.0)
zetas = (0.0, -17.0 / 60.0, -5.0 / 12.0)


def extended(shard, sides, width):
    for axis, dim in sides:
        count, length = (lax.axis_size(axis), shard.shape[dim])
        up = [(i, (i + 1) % count) for i in range(count)]
        down = [(j, i) for i, j in up]
        last = lax.slice_in_dim(shard, length - width, length, axis=dim)
        first = lax.slice_in_dim(shard, 0, width, axis=dim)
        before = lax.ppermute(last, axis, up)
        after = lax.ppermute(first, axis, down)
        shard = jnp.concatenate([before, shard, after], axis=dim)
    return shard


def tendency(center, along_x, along_z, spacing):
    back_far, back_near, ahead_near, ahead_far = along_x
    side_far, side_near, front_near, front_far = along_z
    lower_gap = spacing[:-1]
    upper_gap = spacing[1:]
    padded_y = jnp.pad(center, ((0, 0), (0, 0), (0, 0), (1, 1)))
    beneath = padded_y[..., :-2]
    overhead = padded_y[..., 2:]
    grad_x = (8.0 * (ahead_near - back_near) - (ahead_far - back_far)) / 12.0
    grad_z = (8.0 * (front_near - side_near) - (front_far - side_far)) / 12.0
    grad_y = (overhead - beneath) / (lower_gap + upper_gap)
    curv_x = (-ahead_far + 16.0 * ahead_near - 30.0 * center + 16.0 * back_near - back_far) / 12.0
    curv_z = (-front_far + 16.0 * front_near - 30.0 * center + 16.0 * side_near - side_far) / 12.0
    curv_y = (
        2.0
        * ((overhead - center) / upper_gap - (center - beneath) / lower_gap)
        / (lower_gap + upper_gap)
    )
    advect = center[0:1] * grad_x + center[1:2] * grad_y + center[2:3] * grad_z
    push = jnp.array([forcing, 0.0, 0.0], jnp.float32)[:, None, None, None]
    return -advect + viscosity * (curv_x + curv_y + curv_z) + push


def inner(left, right):
    return lax.dot_general(
        left, right, (((1,), (1,)), ((), ())), preferred_element_type=jnp.float32
    )


def exact_dot(left, right):
    return jnp.dot(left, right, precision=lax.Precision.HIGHEST)


places = {(i, j): (i, j) for i in range(4) for j in range(i, 4)}
places.update({(4, 4): (1, 0), (2, 4): (2, 0), (3, 4): (2, 1), (0, 4): (3, 0), (1, 4): (3, 1)})


def factor_kernel(packed_ref, factor_ref, left_ref, right_ref, work, side):
    f32 = jnp.float32
    lanes8 = lax.broadcasted_iota(jnp.int32, (8, 128), 1)
    subs8 = lax.broadcasted_iota(jnp.int32, (8, 128), 0)
    lanes = lax.broadcasted_iota(jnp.int32, (32, 128), 1)
    rows = lax.broadcasted_iota(jnp.int32, (32, 128), 0)
    for p in range(4):
        piece = packed_ref[32 * p : 32 * p + 32, :]
        work[32 * p : 32 * p + 32, :] = jnp.where(lanes >= 32 * p, piece, 0.0)
        r, c = places[(p, 4)]
        last = packed_ref[32 * r : 32 * r + 32, :]
        if c:
            last = pltpu.roll(last, 128 - 32 * c, 1)
        side[32 * p : 32 * p + 32, :] = jnp.where(lanes < 32, last, 0.0)
    r, c = places[(4, 4)]
    work[128:160, :] = jnp.zeros((32, 128), f32)
    side[128:160, :] = jnp.where(lanes < 32, packed_ref[32 * r : 32 * r + 32, :], 0.0)

    for p in range(5):
        base = 32 * p
        main = [work[base + 8 * g : base + 8 * g + 8, :] for g in range(4)]
        tail = [side[base + 8 * g : base + 8 * g + 8, :] for g in range(4)]
        scale = [None] * 4
        for gk in range(4):
            own, other = (main, tail) if p < 4 else (tail, main)
            first = (base if p < 4 else 0) + 8 * gk
            spread = lambda value, j: jnp.broadcast_to(value[:, j : j + 1], (8, 128))
            pick = lambda value, i: jnp.broadcast_to(value[i : i + 1, :], (8, 128))
            cols = {g: [spread(own[g], first + j) for j in range(8)] for g in range(gk, 4)}
            low = {(i, j): pick(cols[gk][j], i) for j in range(8) for i in range(j, 8)}
            own_rows = [pick(own[gk], i) for i in range(8)]
            other_rows = [pick(other[gk], i) for i in range(8)]
            inside = (lanes8 >= first) & (lanes8 < first + 8)
            solved_rows = [
                jnp.where(inside, jnp.where(lanes8 == first + i, 1.0, 0.0), own_rows[i])
                for i in range(8)
            ]
            roots = []
            for j in range(8):
                root = lax.rsqrt(low[j, j])
                inv = root * root
                roots.append(root)
                coef = {i: low[i, j] * inv for i in range(j + 1, 8)}
                for i in range(j + 1, 8):
                    for m in range(j + 1, i + 1):
                        low[i, m] = low[i, m] - coef[i] * low[m, j]
                    own_rows[i] = own_rows[i] - coef[i] * own_rows[j]
                    solved_rows[i] = solved_rows[i] - coef[i] * solved_rows[j]
                    other_rows[i] = other_rows[i] - coef[i] * other_rows[j]
                for g in range(gk + 1, 4):
                    for m in range(j + 1, 8):
                        cols[g][m] = cols[g][m] - coef[m] * cols[g][j]
                    factor_col = cols[g][j] * inv
                    if j == 0:
                        own[g] = jnp.where(inside, 0.0, own[g])
                    own[g] = own[g] - factor_col * solved_rows[j]
                    other[g] = other[g] - factor_col * other_rows[j]
            new_own, new_other, new_scale = None, None, None
            for i in range(8):
                mixed = jnp.where(inside & (lanes8 > first + i), own_rows[i], solved_rows[i])
                new_own = mixed if i == 0 else jnp.where(subs8 == i, mixed, new_own)
                new_other = other_rows[i] if i == 0 else jnp.where(subs8 == i, other_rows[i], new_other)
                new_scale = roots[i] if i == 0 else jnp.where(subs8 == i, roots[i], new_scale)
            own[gk], other[gk], scale[gk] = new_own, new_other, new_scale
        mainp = jnp.concatenate(main, axis=0)
        tailp = jnp.concatenate(tail, axis=0)
        scalep = jnp.concatenate(scale, axis=0)
        if p < 4:
            diag = lanes == rows + base
            scaled = mainp * scalep
            upper = jnp.where(lanes > rows + base, scaled, jnp.where(diag, 1.0 / scalep, 0.0))
            full_main = jnp.where((lanes > rows + base) & (lanes < base + 32), 0.0, scaled)
            side_out = tailp * scalep
            factor_ref[base : base + 32, 0:128] = upper
            factor_ref[base : base + 32, 128:160] = side_out[:, 0:32]
            both = jnp.concatenate([upper, side_out], axis=1)
            solved = jnp.concatenate([full_main, side_out], axis=1)
            change = lax.dot_general(
                both, solved, (((0,), (0,)), ((), ())),
                precision=lax.Precision.HIGHEST, preferred_element_type=f32,
            )
            for q in range(p + 1, 5):
                span = slice(32 * q, 32 * q + 32)
                block = (lanes >= base) & (lanes < base + 32)
                work[span, :] = jnp.where(block, 0.0, work[span, :]) - change[span, 0:128]
                side[span, :] = side[span, :] - change[span, 128:256]
        else:
            diag = lanes == rows
            factor_ref[128:160, 0:128] = jnp.zeros((32, 128), f32)
            factor_ref[128:160, 128:160] = jnp.where(
                lanes > rows, tailp * scalep, jnp.where(diag, 1.0 / scalep, 0.0)
            )[:, 0:32]
            left_ref[...] = (mainp * scalep).astype(jnp.bfloat16)
            right_ref[...] = jnp.where(lanes <= rows, tailp * scalep, 0.0).astype(jnp.bfloat16)


def factorize(packed):
    return pl.pallas_call(
        factor_kernel,
        out_shape=(
            jax.ShapeDtypeStruct((160, 160), jnp.float32),
            jax.ShapeDtypeStruct((32, 128), jnp.bfloat16),
            jax.ShapeDtypeStruct((32, 128), jnp.bfloat16),
        ),
        scratch_shapes=[pltpu.VMEM((160, 128), jnp.float32), pltpu.VMEM((160, 128), jnp.float32)],
    )(packed)


def pack(gram):
    out = [[None] * 4 for _ in range(4)]
    for (i, j), (r, c) in places.items():
        out[r][c] = gram[32 * i : 32 * i + 32, 32 * j : 32 * j + 32]
    return jnp.block([[b if b is not None else jnp.zeros((32, 32), jnp.float32) for b in row] for row in out])


def summed(packed):
    count_x, count_z = lax.axis_size("gx"), lax.axis_size("gz")
    pieces = packed.reshape(count_x, -1, 128)
    mine = lax.all_to_all(pieces, "gx", 0, 0).sum(0)
    copies = jnp.broadcast_to(mine[None], (count_z,) + mine.shape)
    mine = lax.all_to_all(copies, "gz", 0, 0).sum(0)
    copies = jnp.broadcast_to(mine[None], (count_x,) + mine.shape)
    return lax.all_to_all(copies, "gx", 0, 0).reshape(packed.shape)


def body(velocity, spacing, basis, history, picks):
    reach = 6
    field = extended(velocity, (("gx", 1), ("gz", 2)), reach)
    previous = jnp.zeros_like(field)
    for section in range(3):
        length_x, length_z = field.shape[1] - 4, field.shape[2] - 4
        center = field[:, 2 : 2 + length_x, 2 : 2 + length_z]
        before = previous[:, 2 : 2 + length_x, 2 : 2 + length_z]
        along_x = tuple(
            (field[:, start : start + length_x, 2 : 2 + length_z] for start in (0, 1, 3, 4))
        )
        along_z = tuple(
            (field[:, 2 : 2 + length_x, start : start + length_z] for start in (0, 1, 3, 4))
        )
        current = tendency(center, along_x, along_z, spacing)
        field = center + step_size * (gammas[section] * current + zetas[section] * before)
        previous = current
    fresh = field.astype(jnp.bfloat16)
    rank = basis.shape[0]
    stored = history.shape[0]
    snaps = picks.shape[0] + 1
    basis_flat = basis.reshape(rank, -1)
    stored_flat = history.reshape(stored, -1)
    fresh_flat = fresh.reshape(1, -1)
    rows = basis_flat.shape[1] * lax.axis_size("gx") * lax.axis_size("gz")
    cross_bb = inner(basis_flat, basis_flat)
    cross_bh = inner(basis_flat, stored_flat)
    cross_bf = inner(basis_flat, fresh_flat)
    cross_hh = inner(stored_flat, stored_flat)
    cross_hf = inner(stored_flat, fresh_flat)
    cross_ff = inner(fresh_flat, fresh_flat)
    full = jnp.block(
        [
            [cross_bb, cross_bh, cross_bf],
            [cross_bh.T, cross_hh, cross_hf],
            [cross_bf.T, cross_hf.T, cross_ff],
        ]
    )
    total = rank + stored + 1
    indices = jnp.concatenate(
        [jnp.arange(rank, dtype=jnp.int32), rank + picks, jnp.array([rank + stored], jnp.int32)]
    )
    select = (indices[:, None] == jnp.arange(total, dtype=jnp.int32)[None, :]).astype(jnp.float32)
    local = exact_dot(exact_dot(select, full), select.T)
    factor, left, right = factorize(summed(pack(local)) / rows)
    part_basis = left.T
    part_snap = right[:, :snaps].T
    placing = (picks[:, None] == jnp.arange(stored, dtype=jnp.int32)[None, :]).astype(jnp.float32)
    stored_coef = exact_dot(placing.T, part_snap[:-1].astype(jnp.float32)).astype(jnp.bfloat16)
    fresh_coef = part_snap[-1:]
    directions = jnp.dot(part_basis.T, basis_flat, preferred_element_type=jnp.float32)
    directions = directions + jnp.dot(
        stored_coef.T, stored_flat, preferred_element_type=jnp.float32
    )
    directions = directions + jnp.dot(fresh_coef.T, fresh_flat, preferred_element_type=jnp.float32)
    directions = directions.astype(jnp.bfloat16).reshape((snaps,) + velocity.shape)
    return (field, factor, directions)


def solution(mesh):
    return jax.shard_map(
        body,
        mesh=mesh,
        in_specs=(
            P(None, "gx", "gz", None),
            P(),
            P(None, None, "gx", "gz", None),
            P(None, None, "gx", "gz", None),
            P(),
        ),
        out_specs=(P(None, "gx", "gz", None), P(), P(None, None, "gx", "gz", None)),
        check_vma=False,
    )
```

```python
import functools

import jax
import jax.numpy as jnp
from jax import lax
from jax.experimental import pallas as pl
from jax.experimental.pallas import tpu as pltpu
from jax.sharding import PartitionSpec as P

step_size = 0.1
viscosity = 0.05
forcing = 0.5
gammas = (8.0 / 15.0, 5.0 / 12.0, 3.0 / 4.0)
zetas = (0.0, -17.0 / 60.0, -5.0 / 12.0)


def neighbours(last, first, axis):
    count = lax.axis_size(axis)
    up = [(i, (i + 1) % count) for i in range(count)]
    down = [(j, i) for i, j in up]
    return lax.ppermute(last, axis, up), lax.ppermute(first, axis, down)


def edges_kernel(own_ref, behind_ref, ahead_ref, padded_ref, last_ref, first_ref):
    padded_ref[...] = own_ref[...]
    padded_ref[:, :, 0:6, :] = behind_ref[:, :, 2:8, :]
    padded_ref[:, :, 14:20, :] = ahead_ref[:, :, 0:6, :]
    for target, starts in ((last_ref, (2, 4, 6)), (first_ref, (4, 2, 0))):
        target[:, :, 0:8, :] = padded_ref[:, starts[0] : starts[0] + 2, 6:14, :]
        target[:, :, 8:20, :] = padded_ref[:, starts[1] : starts[1] + 2, 4:16, :]
        target[:, :, 20:36, :] = padded_ref[:, starts[2] : starts[2] + 2, 2:18, :]


def edges(velocity, behind, ahead):
    return pl.pallas_call(
        edges_kernel,
        in_specs=[whole, whole, whole],
        out_specs=(whole, whole, whole),
        out_shape=(
            jax.ShapeDtypeStruct((3, 8, 24, 128), jnp.float32),
            jax.ShapeDtypeStruct((3, 2, 36, 128), jnp.float32),
            jax.ShapeDtypeStruct((3, 2, 36, 128), jnp.float32),
        ),
        compiler_params=pltpu.CompilerParams(vmem_limit_bytes=8 * 2**20),
        cost_estimate=pl.CostEstimate(flops=0, bytes_accessed=40 * 10**6, transcendentals=0),
    )(velocity, behind, ahead)


def advance(spacing_ref, padded_ref, behind_ref, ahead_ref, field_ref, even, odd, tend):
    even[...] = jnp.zeros(even.shape, jnp.float32)
    odd[...] = jnp.zeros(odd.shape, jnp.float32)
    even[:, 6:14, :, :] = padded_ref[...]
    for source, starts in ((behind_ref, (0, 2, 4)), (ahead_ref, (18, 16, 14))):
        even[:, starts[0] : starts[0] + 2, 6:14, :] = source[:, :, 0:8, :]
        even[:, starts[1] : starts[1] + 2, 4:16, :] = source[:, :, 8:20, :]
        even[:, starts[2] : starts[2] + 2, 2:18, :] = source[:, :, 20:36, :]
    lower, upper = spacing_ref[:, 0:128], spacing_ref[:, 1:129]
    y = lax.broadcasted_iota(jnp.int32, (1, 128), 1)
    slope = 1.0 / (lower + upper)
    slope_up = jnp.where(y < 127, slope, 0.0)
    slope_down = jnp.where(y > 0, slope, 0.0)
    curve_up = 2.0 * slope_up / upper
    curve_down = 2.0 * slope_down / lower
    curve_own = 2.0 * slope * (1.0 / upper + 1.0 / lower) + 5.0

    for section in range(3):
        source = odd if section == 1 else even
        first, count = 2 + 2 * section, 16 - 4 * section
        start, length = (2, 16) if section < 2 else (6, 8)
        span = slice(start, start + length)

        @pl.loop(first, first + count)
        def _(x):
            speed = [source[c, x, span, :] for c in range(3)]
            for c in range(3):
                own = speed[c]
                west, east = source[c, x - 1, span, :], source[c, x + 1, span, :]
                west_far, east_far = source[c, x - 2, span, :], source[c, x + 2, span, :]
                south = source[c, x, start - 1 : start - 1 + length, :]
                north = source[c, x, start + 1 : start + 1 + length, :]
                south_far = source[c, x, start - 2 : start - 2 + length, :]
                north_far = source[c, x, start + 2 : start + 2 + length, :]
                beneath = pltpu.roll(own, 1, 1)
                overhead = pltpu.roll(own, 127, 1)
                grad_x = (8.0 * (east - west) - (east_far - west_far)) * (1.0 / 12.0)
                grad_z = (8.0 * (north - south) - (north_far - south_far)) * (1.0 / 12.0)
                grad_y = overhead * slope_up - beneath * slope_down
                near = (east + west) + (north + south)
                far = (east_far + west_far) + (north_far + south_far)
                curve = (16.0 * near - far) * (1.0 / 12.0)
                curve = curve + overhead * curve_up + beneath * curve_down - own * curve_own
                advect = speed[0] * grad_x + speed[1] * grad_y + speed[2] * grad_z
                rate = viscosity * curve - advect
                if c == 0:
                    rate = rate + forcing
                change = gammas[section] * rate
                if section == 1:
                    change = change + zetas[1] * tend[c, x]
                if section == 2:
                    change = change + zetas[2] * tend[c, x, 4:12, :]
                result = own + step_size * change
                if section < 2:
                    tend[c, x] = rate
                    (even if section == 1 else odd)[c, x, span, :] = result
                else:
                    field_ref[pl.ds(pl.multiple_of((c * 8 + x - 6) * 8, 8), 8), :] = result


places = {(i, j): (i, j) for i in range(4) for j in range(i, 4)}
places.update({(4, 4): (1, 0), (2, 4): (2, 0), (3, 4): (2, 1), (0, 4): (3, 0), (1, 4): (3, 1)})
contract_last = (((1,), (1,)), ((), ()))
whole = pl.BlockSpec(memory_space=pltpu.VMEM)


def load_kernel(basis_ref, stored_ref, modes, snaps, sems):
    copies = []
    for chunk in range(6):
        span = pl.ds(32 * chunk, 32)
        copies += [
            pltpu.make_async_copy(basis_ref.at[:, span, :], modes.at[chunk], sems.at[0, chunk]),
            pltpu.make_async_copy(stored_ref.at[:, span, :], snaps.at[chunk], sems.at[1, chunk]),
        ]
    for copy in copies:
        copy.start()
    for copy in copies:
        copy.wait()


def loaded_parts(basis, stored):
    return pl.pallas_call(
        load_kernel,
        in_specs=[pl.BlockSpec(memory_space=pl.ANY)] * 2,
        out_specs=(whole, whole),
        out_shape=(
            jax.ShapeDtypeStruct((6, 128, 32, 128), jnp.bfloat16),
            jax.ShapeDtypeStruct((6, 40, 32, 128), jnp.bfloat16),
        ),
        scratch_shapes=[pltpu.SemaphoreType.DMA((2, 6))],
        compiler_params=pltpu.CompilerParams(vmem_limit_bytes=42 * 2**20),
        cost_estimate=pl.CostEstimate(flops=0, bytes_accessed=16 * 10**6, transcendentals=0),
    )(basis, stored)


def gram_kernel(
    picks_ref, basis_ref, stored_ref, spacing_ref, padded_ref, behind_ref, ahead_ref,
    packed_ref, turned_ref, fresh_ref, even, odd, tend,
):
    f32, bf16 = jnp.float32, jnp.bfloat16
    advance(spacing_ref, padded_ref, behind_ref, ahead_ref, fresh_ref, even, odd, tend)

    def step(chunk, total):
        for group in range(10):
            for half in range(2):
                rows = slice(16 * half, 16 * half + 16)
                place = pl.ds(pl.multiple_of(32 * chunk + 16 * half, 16), 16)
                if group < 8:
                    tile = basis_ref[chunk, 16 * group : 16 * group + 16, rows, :]
                else:
                    first = 16 * (group - 8)
                    tile = jnp.stack(
                        [
                            stored_ref[chunk, picks_ref[first + j], rows, :]
                            if first + j < 31
                            else fresh_ref[place, :].astype(bf16)
                            for j in range(16)
                        ],
                        axis=0,
                    )
                tile = jnp.swapaxes(tile, 0, 1)
                for s in range(16):
                    lanes = slice(256 * s + 128 * half, 256 * s + 128 * half + 128)
                    turned_ref[chunk, 16 * group : 16 * group + 16, lanes] = tile[s]
        block = turned_ref[chunk]
        return total + lax.dot_general(block, block, contract_last, preferred_element_type=f32)

    total = lax.fori_loop(0, 6, step, jnp.zeros((160, 160), f32))
    lanes = lax.broadcasted_iota(jnp.int32, (32, 128), 1)
    right = jnp.concatenate([total[:, 128:160], jnp.zeros((160, 96), f32)], axis=1)
    parts = [jnp.where(lanes >= 32 * p, total[32 * p : 32 * p + 32, 0:128], 0.0) for p in range(4)]
    for p in range(5):
        r, c = places[(p, 4)]
        part = right[32 * p : 32 * p + 32, :]
        parts[r] = parts[r] + (pltpu.roll(part, 32 * c, 1) if c else part)
    for r in range(16):
        packed_ref[:, 128 * r : 128 * r + 128] = parts[r // 4][8 * (r % 4) : 8 * (r % 4) + 8, :]


def local_gram(picks, *operands):
    return pl.pallas_call(
        gram_kernel,
        in_specs=[pl.BlockSpec(memory_space=pltpu.SMEM)] + [whole] * 6,
        out_specs=(whole, whole, whole),
        out_shape=(
            jax.ShapeDtypeStruct((8, 2048), jnp.float32),
            jax.ShapeDtypeStruct((6, 160, 4096), jnp.bfloat16),
            jax.ShapeDtypeStruct((192, 128), jnp.float32),
        ),
        scratch_shapes=[
            pltpu.VMEM((3, 20, 24, 128), jnp.float32),
            pltpu.VMEM((3, 20, 24, 128), jnp.float32),
            pltpu.VMEM((3, 20, 16, 128), jnp.float32),
        ],
        compiler_params=pltpu.CompilerParams(vmem_limit_bytes=16 * 2**20),
        cost_estimate=pl.CostEstimate(flops=2 * 10**9, bytes_accessed=16 * 10**6, transcendentals=0),
    )(picks, *operands)


def factor_kernel(rows_total, sums_ref, factor_ref, left_ref, right_ref, work, side):
    f32 = jnp.float32
    lanes8 = lax.broadcasted_iota(jnp.int32, (8, 128), 1)
    subs8 = lax.broadcasted_iota(jnp.int32, (8, 128), 0)
    lanes = lax.broadcasted_iota(jnp.int32, (32, 128), 1)
    rows = lax.broadcasted_iota(jnp.int32, (32, 128), 0)
    def loaded(r):
        tiles = [
            jnp.concatenate([sums_ref[j, :, 128 * q : 128 * q + 128] for j in range(8)], axis=0)
            for q in range(4 * r, 4 * r + 4)
        ]
        return jnp.concatenate(tiles, axis=0) / rows_total

    gathered = [loaded(r) for r in range(4)]
    for p in range(4):
        work[32 * p : 32 * p + 32, :] = jnp.where(lanes >= 32 * p, gathered[p], 0.0)
        r, c = places[(p, 4)]
        last = pltpu.roll(gathered[r], 128 - 32 * c, 1) if c else gathered[r]
        side[32 * p : 32 * p + 32, :] = jnp.where(lanes < 32, last, 0.0)
    work[128:160, :] = jnp.zeros((32, 128), f32)
    last = gathered[places[(4, 4)][0]]
    side[128:160, :] = jnp.where(lanes < 32, last, 0.0)

    for p in range(5):
        base = 32 * p
        main = [work[base + 8 * g : base + 8 * g + 8, :] for g in range(4)]
        tail = [side[base + 8 * g : base + 8 * g + 8, :] for g in range(4)]
        scale = [None] * 4
        for gk in range(4):
            own, other = (main, tail) if p < 4 else (tail, main)
            first = (base if p < 4 else 0) + 8 * gk
            spread = lambda value, j: jnp.broadcast_to(value[:, j : j + 1], (8, 128))
            pick = lambda value, i: jnp.broadcast_to(value[i : i + 1, :], (8, 128))
            cols = {g: [spread(own[g], first + j) for j in range(8)] for g in range(gk, 4)}
            low = {(i, j): pick(cols[gk][j], i) for j in range(8) for i in range(j, 8)}
            own_rows = [pick(own[gk], i) for i in range(8)]
            other_rows = [pick(other[gk], i) for i in range(8)]
            inside = (lanes8 >= first) & (lanes8 < first + 8)
            solved_rows = [
                jnp.where(inside, jnp.where(lanes8 == first + i, 1.0, 0.0), own_rows[i])
                for i in range(8)
            ]
            roots = []
            for j in range(8):
                root = lax.rsqrt(low[j, j])
                inv = root * root
                roots.append(root)
                coef = {i: low[i, j] * inv for i in range(j + 1, 8)}
                for i in range(j + 1, 8):
                    for m in range(j + 1, i + 1):
                        low[i, m] = low[i, m] - coef[i] * low[m, j]
                    own_rows[i] = own_rows[i] - coef[i] * own_rows[j]
                    solved_rows[i] = solved_rows[i] - coef[i] * solved_rows[j]
                    other_rows[i] = other_rows[i] - coef[i] * other_rows[j]
                for g in range(gk + 1, 4):
                    for m in range(j + 1, 8):
                        cols[g][m] = cols[g][m] - coef[m] * cols[g][j]
                    factor_col = cols[g][j] * inv
                    if j == 0:
                        own[g] = jnp.where(inside, 0.0, own[g])
                    own[g] = own[g] - factor_col * solved_rows[j]
                    other[g] = other[g] - factor_col * other_rows[j]
            new_own, new_other, new_scale = None, None, None
            for i in range(8):
                mixed = jnp.where(inside & (lanes8 > first + i), own_rows[i], solved_rows[i])
                new_own = mixed if i == 0 else jnp.where(subs8 == i, mixed, new_own)
                new_other = other_rows[i] if i == 0 else jnp.where(subs8 == i, other_rows[i], new_other)
                new_scale = roots[i] if i == 0 else jnp.where(subs8 == i, roots[i], new_scale)
            own[gk], other[gk], scale[gk] = new_own, new_other, new_scale
        mainp = jnp.concatenate(main, axis=0)
        tailp = jnp.concatenate(tail, axis=0)
        scalep = jnp.concatenate(scale, axis=0)
        if p < 4:
            diag = lanes == rows + base
            scaled = mainp * scalep
            upper = jnp.where(lanes > rows + base, scaled, jnp.where(diag, 1.0 / scalep, 0.0))
            full_main = jnp.where((lanes > rows + base) & (lanes < base + 32), 0.0, scaled)
            side_out = tailp * scalep
            factor_ref[base : base + 32, 0:128] = upper
            factor_ref[base : base + 32, 128:160] = side_out[:, 0:32]
            both = jnp.concatenate([upper, side_out], axis=1)
            solved = jnp.concatenate([full_main, side_out], axis=1)
            change = lax.dot_general(
                both, solved, (((0,), (0,)), ((), ())),
                precision=lax.Precision.HIGHEST, preferred_element_type=f32,
            )
            for q in range(p + 1, 5):
                span = slice(32 * q, 32 * q + 32)
                block = (lanes >= base) & (lanes < base + 32)
                work[span, :] = jnp.where(block, 0.0, work[span, :]) - change[span, 0:128]
                side[span, :] = side[span, :] - change[span, 128:256]
        else:
            diag = lanes == rows
            factor_ref[128:160, 0:128] = jnp.zeros((32, 128), f32)
            factor_ref[128:160, 128:160] = jnp.where(
                lanes > rows, tailp * scalep, jnp.where(diag, 1.0 / scalep, 0.0)
            )[:, 0:32]
            left_ref[...] = (mainp * scalep).astype(jnp.bfloat16)
            right_ref[...] = jnp.where(lanes <= rows, tailp * scalep, 0.0).astype(jnp.bfloat16)


def spread(left_ref, right_ref, turned_ref, out_ref, result, sems):
    f32, bf16 = jnp.float32, jnp.bfloat16
    coef = jnp.concatenate([left_ref[...], right_ref[:, 0:32]], axis=1)

    def copy(chunk):
        span = pl.ds(pl.multiple_of(32 * chunk, 32), 32)
        return pltpu.make_async_copy(result.at[chunk], out_ref.at[:, span, :], sems.at[chunk])

    @pl.loop(0, 6)
    def _(chunk):
        total = jnp.dot(coef, turned_ref[chunk], preferred_element_type=f32).astype(bf16)
        for group in range(2):
            for half in range(2):
                tile = jnp.stack(
                    [
                        total[16 * group : 16 * group + 16, 256 * s + 128 * half : 256 * s + 128 * half + 128]
                        for s in range(16)
                    ],
                    axis=0,
                )
                result[chunk, 16 * group : 16 * group + 16, 16 * half : 16 * half + 16, :] = jnp.swapaxes(tile, 0, 1)
        copy(chunk).start()

    @pl.loop(0, 6)
    def _(chunk):
        copy(chunk).wait()


def last_kernel(
    rows_total, sums_ref, turned_ref, factor_ref, out_ref, work, side, left, right, result, sems
):
    factor_kernel(rows_total, sums_ref, factor_ref, left, right, work, side)
    spread(left, right, turned_ref, out_ref, result, sems)


def finish(sums, turned, rows_total):
    return pl.pallas_call(
        functools.partial(last_kernel, rows_total),
        in_specs=[whole, whole],
        out_specs=(whole, pl.BlockSpec(memory_space=pl.ANY)),
        out_shape=(
            jax.ShapeDtypeStruct((160, 160), jnp.float32),
            jax.ShapeDtypeStruct((32, 192, 128), jnp.bfloat16),
        ),
        scratch_shapes=[
            pltpu.VMEM((160, 128), jnp.float32),
            pltpu.VMEM((160, 128), jnp.float32),
            pltpu.VMEM((32, 128), jnp.bfloat16),
            pltpu.VMEM((32, 128), jnp.bfloat16),
            pltpu.VMEM((6, 32, 32, 128), jnp.bfloat16),
            pltpu.SemaphoreType.DMA((6,)),
        ],
        compiler_params=pltpu.CompilerParams(vmem_limit_bytes=16 * 2**20),
    )(sums, turned)


def everyone(value, axis):
    count = lax.axis_size(axis)
    copies = jnp.broadcast_to(value.reshape(1, 1, -1), (count, 1, value.size))
    return lax.all_to_all(copies, axis, 0, 0)


def added(pieces):
    return functools.reduce(jnp.add, [pieces[i] for i in range(pieces.shape[0])])


def body(velocity, spacing, basis, history, picks):
    modes, stored = basis.shape[0], history.shape[0]
    rows_total = float(velocity.size * lax.axis_size("gx") * lax.axis_size("gz"))
    behind, ahead = neighbours(velocity, velocity[:, :, 0:6], "gz")
    own = jnp.pad(velocity, ((0, 0), (0, 0), (6, 10), (0, 0)))
    padded, last, first = edges(own, behind, ahead)
    behind, ahead = neighbours(last, first, "gx")
    packed, turned, field = local_gram(
        picks,
        *loaded_parts(basis.reshape(modes, -1, 128), history.reshape(stored, -1, 128)),
        spacing.reshape(1, -1),
        padded,
        behind,
        ahead,
    )
    mine = added(lax.all_to_all(packed.reshape(8, 1, -1), "gx", 0, 0))
    mine = added(everyone(mine, "gz"))
    factor, directions = finish(everyone(mine, "gx"), turned, rows_total)
    return (field.reshape(velocity.shape), factor, directions.reshape((32,) + velocity.shape))


def solution(mesh):
    return jax.shard_map(
        body,
        mesh=mesh,
        in_specs=(
            P(None, "gx", "gz", None),
            P(),
            P(None, None, "gx", "gz", None),
            P(None, None, "gx", "gz", None),
            P(),
        ),
        out_specs=(P(None, "gx", "gz", None), P(), P(None, None, "gx", "gz", None)),
        check_vma=False,
    )
```

```python
import functools

import jax
import jax.numpy as jnp
from jax import lax
from jax.experimental import pallas as pl
from jax.experimental.pallas import tpu as pltpu
from jax.sharding import PartitionSpec as P

step_size = 0.1
viscosity = 0.05
forcing = 0.5
gammas = (8.0 / 15.0, 5.0 / 12.0, 3.0 / 4.0)
zetas = (0.0, -17.0 / 60.0, -5.0 / 12.0)


def neighbours(last, first, axis):
    count = lax.axis_size(axis)
    up = [(i, (i + 1) % count) for i in range(count)]
    down = [(j, i) for i, j in up]
    return lax.ppermute(last, axis, up), lax.ppermute(first, axis, down)


def edges_kernel(own_ref, behind_ref, ahead_ref, padded_ref, last_ref, first_ref):
    padded_ref[...] = own_ref[...]
    padded_ref[:, :, 0:6, :] = behind_ref[:, :, 2:8, :]
    padded_ref[:, :, 14:20, :] = ahead_ref[:, :, 0:6, :]
    for target, starts in ((last_ref, (2, 4, 6)), (first_ref, (4, 2, 0))):
        target[:, :, 0:8, :] = padded_ref[:, starts[0] : starts[0] + 2, 6:14, :]
        target[:, :, 8:20, :] = padded_ref[:, starts[1] : starts[1] + 2, 4:16, :]
        target[:, :, 20:36, :] = padded_ref[:, starts[2] : starts[2] + 2, 2:18, :]


def edges(velocity, behind, ahead):
    return pl.pallas_call(
        edges_kernel,
        in_specs=[whole, whole, whole],
        out_specs=(whole, whole, whole),
        out_shape=(
            jax.ShapeDtypeStruct((3, 8, 24, 128), jnp.float32),
            jax.ShapeDtypeStruct((3, 2, 36, 128), jnp.float32),
            jax.ShapeDtypeStruct((3, 2, 36, 128), jnp.float32),
        ),
        compiler_params=pltpu.CompilerParams(vmem_limit_bytes=8 * 2**20),
        cost_estimate=pl.CostEstimate(flops=0, bytes_accessed=40 * 10**6, transcendentals=0),
    )(velocity, behind, ahead)


def advance(spacing_ref, padded_ref, behind_ref, ahead_ref, field_ref, even, odd, tend):
    even[...] = jnp.zeros(even.shape, jnp.float32)
    odd[...] = jnp.zeros(odd.shape, jnp.float32)
    even[:, 6:14, :, :] = padded_ref[...]
    for source, starts in ((behind_ref, (0, 2, 4)), (ahead_ref, (18, 16, 14))):
        even[:, starts[0] : starts[0] + 2, 6:14, :] = source[:, :, 0:8, :]
        even[:, starts[1] : starts[1] + 2, 4:16, :] = source[:, :, 8:20, :]
        even[:, starts[2] : starts[2] + 2, 2:18, :] = source[:, :, 20:36, :]
    lower, upper = spacing_ref[:, 0:128], spacing_ref[:, 1:129]
    y = lax.broadcasted_iota(jnp.int32, (1, 128), 1)
    slope = 1.0 / (lower + upper)
    slope_up = jnp.where(y < 127, slope, 0.0)
    slope_down = jnp.where(y > 0, slope, 0.0)
    curve_up = 2.0 * slope_up / upper
    curve_down = 2.0 * slope_down / lower
    curve_own = 2.0 * slope * (1.0 / upper + 1.0 / lower) + 5.0

    for section in range(3):
        source = odd if section == 1 else even
        first, count = 2 + 2 * section, 16 - 4 * section
        start, length = (2, 16) if section < 2 else (6, 8)
        span = slice(start, start + length)

        @pl.loop(first, first + count, unroll=4)
        def _(x):
            speed = [source[c, x, span, :] for c in range(3)]
            for c in range(3):
                own = speed[c]
                west, east = source[c, x - 1, span, :], source[c, x + 1, span, :]
                west_far, east_far = source[c, x - 2, span, :], source[c, x + 2, span, :]
                south = source[c, x, start - 1 : start - 1 + length, :]
                north = source[c, x, start + 1 : start + 1 + length, :]
                south_far = source[c, x, start - 2 : start - 2 + length, :]
                north_far = source[c, x, start + 2 : start + 2 + length, :]
                beneath = pltpu.roll(own, 1, 1)
                overhead = pltpu.roll(own, 127, 1)
                grad_x = (8.0 * (east - west) - (east_far - west_far)) * (1.0 / 12.0)
                grad_z = (8.0 * (north - south) - (north_far - south_far)) * (1.0 / 12.0)
                grad_y = overhead * slope_up - beneath * slope_down
                near = (east + west) + (north + south)
                far = (east_far + west_far) + (north_far + south_far)
                curve = (16.0 * near - far) * (1.0 / 12.0)
                curve = curve + overhead * curve_up + beneath * curve_down - own * curve_own
                advect = speed[0] * grad_x + speed[1] * grad_y + speed[2] * grad_z
                rate = viscosity * curve - advect
                if c == 0:
                    rate = rate + forcing
                change = gammas[section] * rate
                if section == 1:
                    change = change + zetas[1] * tend[c, x]
                if section == 2:
                    change = change + zetas[2] * tend[c, x, 4:12, :]
                result = own + step_size * change
                if section < 2:
                    tend[c, x] = rate
                    (even if section == 1 else odd)[c, x, span, :] = result
                else:
                    field_ref[pl.ds(pl.multiple_of((c * 8 + x - 6) * 8, 8), 8), :] = result


places = {(i, j): (i, j) for i in range(4) for j in range(i, 4)}
places.update({(4, 4): (1, 0), (2, 4): (2, 0), (3, 4): (2, 1), (0, 4): (3, 0), (1, 4): (3, 1)})
contract_last = (((1,), (1,)), ((), ()))
whole = pl.BlockSpec(memory_space=pltpu.VMEM)


def load_kernel(basis_ref, stored_ref, modes, snaps, sems):
    copies = []
    for chunk in range(6):
        span = pl.ds(32 * chunk, 32)
        copies += [
            pltpu.make_async_copy(basis_ref.at[:, span, :], modes.at[chunk], sems.at[0, chunk]),
            pltpu.make_async_copy(stored_ref.at[:, span, :], snaps.at[chunk], sems.at[1, chunk]),
        ]
    for copy in copies:
        copy.start()
    for copy in copies:
        copy.wait()


def loaded_parts(basis, stored):
    return pl.pallas_call(
        load_kernel,
        in_specs=[pl.BlockSpec(memory_space=pl.ANY)] * 2,
        out_specs=(whole, whole),
        out_shape=(
            jax.ShapeDtypeStruct((6, 128, 32, 128), jnp.bfloat16),
            jax.ShapeDtypeStruct((6, 40, 32, 128), jnp.bfloat16),
        ),
        scratch_shapes=[pltpu.SemaphoreType.DMA((2, 6))],
        compiler_params=pltpu.CompilerParams(vmem_limit_bytes=42 * 2**20),
        cost_estimate=pl.CostEstimate(flops=0, bytes_accessed=16 * 10**6, transcendentals=0),
    )(basis, stored)


def gram_kernel(
    picks_ref, basis_ref, stored_ref, spacing_ref, padded_ref, behind_ref, ahead_ref,
    packed_ref, turned_ref, fresh_ref, even, odd, tend,
):
    f32, bf16 = jnp.float32, jnp.bfloat16
    advance(spacing_ref, padded_ref, behind_ref, ahead_ref, fresh_ref, even, odd, tend)

    def step(chunk, total):
        for group in range(10):
            for half in range(2):
                rows = slice(16 * half, 16 * half + 16)
                place = slice(32 * chunk + 16 * half, 32 * chunk + 16 * half + 16)
                if group < 8:
                    tile = basis_ref[chunk, 16 * group : 16 * group + 16, rows, :]
                else:
                    first = 16 * (group - 8)
                    tile = jnp.stack(
                        [
                            stored_ref[chunk, picks_ref[first + j], rows, :]
                            if first + j < 31
                            else fresh_ref[place, :].astype(bf16)
                            for j in range(16)
                        ],
                        axis=0,
                    )
                tile = jnp.swapaxes(tile, 0, 1)
                for s in range(16):
                    lanes = slice(256 * s + 128 * half, 256 * s + 128 * half + 128)
                    turned_ref[chunk, 16 * group : 16 * group + 16, lanes] = tile[s]
        block = turned_ref[chunk]
        return total + lax.dot_general(block, block, contract_last, preferred_element_type=f32)

    total = jnp.zeros((160, 160), f32)
    for chunk in range(6):
        total = step(chunk, total)
    lanes = lax.broadcasted_iota(jnp.int32, (32, 128), 1)
    right = jnp.concatenate([total[:, 128:160], jnp.zeros((160, 96), f32)], axis=1)
    parts = [jnp.where(lanes >= 32 * p, total[32 * p : 32 * p + 32, 0:128], 0.0) for p in range(4)]
    for p in range(5):
        r, c = places[(p, 4)]
        part = right[32 * p : 32 * p + 32, :]
        parts[r] = parts[r] + (pltpu.roll(part, 32 * c, 1) if c else part)
    for r in range(16):
        packed_ref[:, 128 * r : 128 * r + 128] = parts[r // 4][8 * (r % 4) : 8 * (r % 4) + 8, :]


def local_gram(picks, *operands):
    return pl.pallas_call(
        gram_kernel,
        in_specs=[pl.BlockSpec(memory_space=pltpu.SMEM)] + [whole] * 6,
        out_specs=(whole, whole, whole),
        out_shape=(
            jax.ShapeDtypeStruct((8, 2048), jnp.float32),
            jax.ShapeDtypeStruct((6, 160, 4096), jnp.bfloat16),
            jax.ShapeDtypeStruct((192, 128), jnp.float32),
        ),
        scratch_shapes=[
            pltpu.VMEM((3, 20, 24, 128), jnp.float32),
            pltpu.VMEM((3, 20, 24, 128), jnp.float32),
            pltpu.VMEM((3, 20, 16, 128), jnp.float32),
        ],
        compiler_params=pltpu.CompilerParams(vmem_limit_bytes=16 * 2**20),
        cost_estimate=pl.CostEstimate(flops=2 * 10**9, bytes_accessed=16 * 10**6, transcendentals=0),
    )(picks, *operands)


def factor_kernel(rows_total, sums_ref, factor_ref, left_ref, right_ref, work, side):
    f32 = jnp.float32
    lanes8 = lax.broadcasted_iota(jnp.int32, (8, 128), 1)
    subs8 = lax.broadcasted_iota(jnp.int32, (8, 128), 0)
    lanes = lax.broadcasted_iota(jnp.int32, (32, 128), 1)
    rows = lax.broadcasted_iota(jnp.int32, (32, 128), 0)
    def loaded(r):
        tiles = [
            jnp.concatenate([sums_ref[j, :, 128 * q : 128 * q + 128] for j in range(8)], axis=0)
            for q in range(4 * r, 4 * r + 4)
        ]
        return jnp.concatenate(tiles, axis=0) / rows_total

    gathered = [loaded(r) for r in range(4)]
    for p in range(4):
        work[32 * p : 32 * p + 32, :] = jnp.where(lanes >= 32 * p, gathered[p], 0.0)
        r, c = places[(p, 4)]
        last = pltpu.roll(gathered[r], 128 - 32 * c, 1) if c else gathered[r]
        side[32 * p : 32 * p + 32, :] = jnp.where(lanes < 32, last, 0.0)
    work[128:160, :] = jnp.zeros((32, 128), f32)
    last = gathered[places[(4, 4)][0]]
    side[128:160, :] = jnp.where(lanes < 32, last, 0.0)

    for p in range(5):
        base = 32 * p
        main = [work[base + 8 * g : base + 8 * g + 8, :] for g in range(4)]
        tail = [side[base + 8 * g : base + 8 * g + 8, :] for g in range(4)]
        scale = [None] * 4
        for gk in range(4):
            own, other = (main, tail) if p < 4 else (tail, main)
            first = (base if p < 4 else 0) + 8 * gk
            spread = lambda value, j: jnp.broadcast_to(value[:, j : j + 1], (8, 128))
            pick = lambda value, i: jnp.broadcast_to(value[i : i + 1, :], (8, 128))
            cols = {g: [spread(own[g], first + j) for j in range(8)] for g in range(gk, 4)}
            low = {(i, j): pick(cols[gk][j], i) for j in range(8) for i in range(j, 8)}
            own_rows = [pick(own[gk], i) for i in range(8)]
            other_rows = [pick(other[gk], i) for i in range(8)]
            inside = (lanes8 >= first) & (lanes8 < first + 8)
            solved_rows = [
                jnp.where(inside, jnp.where(lanes8 == first + i, 1.0, 0.0), own_rows[i])
                for i in range(8)
            ]
            roots = []
            for j in range(8):
                root = lax.rsqrt(low[j, j])
                inv = root * root
                roots.append(root)
                coef = {i: low[i, j] * inv for i in range(j + 1, 8)}
                for i in range(j + 1, 8):
                    for m in range(j + 1, i + 1):
                        low[i, m] = low[i, m] - coef[i] * low[m, j]
                    own_rows[i] = own_rows[i] - coef[i] * own_rows[j]
                    solved_rows[i] = solved_rows[i] - coef[i] * solved_rows[j]
                    other_rows[i] = other_rows[i] - coef[i] * other_rows[j]
                for g in range(gk + 1, 4):
                    for m in range(j + 1, 8):
                        cols[g][m] = cols[g][m] - coef[m] * cols[g][j]
                    factor_col = cols[g][j] * inv
                    if j == 0:
                        own[g] = jnp.where(inside, 0.0, own[g])
                    own[g] = own[g] - factor_col * solved_rows[j]
                    other[g] = other[g] - factor_col * other_rows[j]
            new_own, new_other, new_scale = None, None, None
            for i in range(8):
                mixed = jnp.where(inside & (lanes8 > first + i), own_rows[i], solved_rows[i])
                new_own = mixed if i == 0 else jnp.where(subs8 == i, mixed, new_own)
                new_other = other_rows[i] if i == 0 else jnp.where(subs8 == i, other_rows[i], new_other)
                new_scale = roots[i] if i == 0 else jnp.where(subs8 == i, roots[i], new_scale)
            own[gk], other[gk], scale[gk] = new_own, new_other, new_scale
        mainp = jnp.concatenate(main, axis=0)
        tailp = jnp.concatenate(tail, axis=0)
        scalep = jnp.concatenate(scale, axis=0)
        if p < 4:
            diag = lanes == rows + base
            scaled = mainp * scalep
            upper = jnp.where(lanes > rows + base, scaled, jnp.where(diag, 1.0 / scalep, 0.0))
            full_main = jnp.where((lanes > rows + base) & (lanes < base + 32), 0.0, scaled)
            side_out = tailp * scalep
            factor_ref[base : base + 32, 0:128] = upper
            factor_ref[base : base + 32, 128:160] = side_out[:, 0:32]
            both = jnp.concatenate([upper, side_out], axis=1)
            solved = jnp.concatenate([full_main, side_out], axis=1)
            block = (lanes >= base) & (lanes < base + 32)

            def reduce_rows(start, stop):
                change = lax.dot_general(
                    both[:, start:stop], solved, (((0,), (0,)), ((), ())),
                    precision=lax.Precision.HIGHEST, preferred_element_type=f32,
                )
                for q in range(start // 32, stop // 32):
                    span = slice(32 * q, 32 * q + 32)
                    part = change[32 * q - start : 32 * q - start + 32, :]
                    work[span, :] = jnp.where(block, 0.0, work[span, :]) - part[:, 0:128]
                    side[span, :] = side[span, :] - part[:, 128:256]

            reduce_rows(base + 32, base + 64)
            if p < 3:
                reduce_rows(base + 64, 160)
        else:
            diag = lanes == rows
            factor_ref[128:160, 0:128] = jnp.zeros((32, 128), f32)
            factor_ref[128:160, 128:160] = jnp.where(
                lanes > rows, tailp * scalep, jnp.where(diag, 1.0 / scalep, 0.0)
            )[:, 0:32]
            left_ref[...] = (mainp * scalep).astype(jnp.bfloat16)
            right_ref[...] = jnp.where(lanes <= rows, tailp * scalep, 0.0).astype(jnp.bfloat16)


def spread(left_ref, right_ref, turned_ref, out_ref, result, sems):
    f32, bf16 = jnp.float32, jnp.bfloat16
    coef = jnp.concatenate([left_ref[...], right_ref[:, 0:32]], axis=1)

    def copy(chunk):
        span = pl.ds(pl.multiple_of(32 * chunk, 32), 32)
        return pltpu.make_async_copy(result.at[chunk], out_ref.at[:, span, :], sems.at[chunk])

    @pl.loop(0, 6, unroll=3)
    def _(chunk):
        total = jnp.dot(coef, turned_ref[chunk], preferred_element_type=f32).astype(bf16)
        for group in range(2):
            for half in range(2):
                tile = jnp.stack(
                    [
                        total[16 * group : 16 * group + 16, 256 * s + 128 * half : 256 * s + 128 * half + 128]
                        for s in range(16)
                    ],
                    axis=0,
                )
                result[chunk, 16 * group : 16 * group + 16, 16 * half : 16 * half + 16, :] = jnp.swapaxes(tile, 0, 1)
        copy(chunk).start()

    @pl.loop(0, 6)
    def _(chunk):
        copy(chunk).wait()


def last_kernel(
    rows_total, sums_ref, turned_ref, factor_ref, out_ref, work, side, left, right, result, sems
):
    factor_kernel(rows_total, sums_ref, factor_ref, left, right, work, side)
    spread(left, right, turned_ref, out_ref, result, sems)


def finish(sums, turned, rows_total):
    return pl.pallas_call(
        functools.partial(last_kernel, rows_total),
        in_specs=[whole, whole],
        out_specs=(whole, pl.BlockSpec(memory_space=pl.ANY)),
        out_shape=(
            jax.ShapeDtypeStruct((160, 160), jnp.float32),
            jax.ShapeDtypeStruct((32, 192, 128), jnp.bfloat16),
        ),
        scratch_shapes=[
            pltpu.VMEM((160, 128), jnp.float32),
            pltpu.VMEM((160, 128), jnp.float32),
            pltpu.VMEM((32, 128), jnp.bfloat16),
            pltpu.VMEM((32, 128), jnp.bfloat16),
            pltpu.VMEM((6, 32, 32, 128), jnp.bfloat16),
            pltpu.SemaphoreType.DMA((6,)),
        ],
        compiler_params=pltpu.CompilerParams(vmem_limit_bytes=16 * 2**20),
    )(sums, turned)


def everyone(value, axis):
    count = lax.axis_size(axis)
    copies = jnp.broadcast_to(value.reshape(1, 1, -1), (count, 1, value.size))
    return lax.all_to_all(copies, axis, 0, 0)


def added(pieces):
    return functools.reduce(jnp.add, [pieces[i] for i in range(pieces.shape[0])])


def body(velocity, spacing, basis, history, picks):
    modes, stored = basis.shape[0], history.shape[0]
    rows_total = float(velocity.size * lax.axis_size("gx") * lax.axis_size("gz"))
    behind, ahead = neighbours(velocity, velocity[:, :, 0:6], "gz")
    own = jnp.pad(velocity, ((0, 0), (0, 0), (6, 10), (0, 0)))
    padded, last, first = edges(own, behind, ahead)
    behind, ahead = neighbours(last, first, "gx")
    packed, turned, field = local_gram(
        picks,
        *loaded_parts(basis.reshape(modes, -1, 128), history.reshape(stored, -1, 128)),
        spacing.reshape(1, -1),
        padded,
        behind,
        ahead,
    )
    mine = added(lax.all_to_all(packed.reshape(8, 1, -1), "gx", 0, 0))
    mine = added(everyone(mine, "gz"))
    factor, directions = finish(everyone(mine, "gx"), turned, rows_total)
    return (field.reshape(velocity.shape), factor, directions.reshape((32,) + velocity.shape))


def solution(mesh):
    return jax.shard_map(
        body,
        mesh=mesh,
        in_specs=(
            P(None, "gx", "gz", None),
            P(),
            P(None, None, "gx", "gz", None),
            P(None, None, "gx", "gz", None),
            P(),
        ),
        out_specs=(P(None, "gx", "gz", None), P(), P(None, None, "gx", "gz", None)),
        check_vma=False,
    )
```

```python
import functools

import jax
import jax.numpy as jnp
from jax import lax
from jax.experimental import pallas as pl
from jax.experimental.pallas import tpu as pltpu
from jax.sharding import PartitionSpec as P

step_size = 0.1
viscosity = 0.05
forcing = 0.5
gammas = (8.0 / 15.0, 5.0 / 12.0, 3.0 / 4.0)
zetas = (0.0, -17.0 / 60.0, -5.0 / 12.0)


def neighbours(last, first, axis):
    count = lax.axis_size(axis)
    up = [(i, (i + 1) % count) for i in range(count)]
    down = [(j, i) for i, j in up]
    return lax.ppermute(last, axis, up), lax.ppermute(first, axis, down)


def edges_kernel(own_ref, behind_ref, ahead_ref, padded_ref, last_ref, first_ref):
    padded_ref[...] = own_ref[...]
    padded_ref[:, :, 0:6, :] = behind_ref[:, :, 2:8, :]
    padded_ref[:, :, 14:20, :] = ahead_ref[:, :, 0:6, :]
    for target, starts in ((last_ref, (2, 4, 6)), (first_ref, (4, 2, 0))):
        target[:, :, 0:8, :] = padded_ref[:, starts[0] : starts[0] + 2, 6:14, :]
        target[:, :, 8:20, :] = padded_ref[:, starts[1] : starts[1] + 2, 4:16, :]
        target[:, :, 20:36, :] = padded_ref[:, starts[2] : starts[2] + 2, 2:18, :]


def edges(velocity, behind, ahead):
    return pl.pallas_call(
        edges_kernel,
        in_specs=[whole, whole, whole],
        out_specs=(whole, whole, whole),
        out_shape=(
            jax.ShapeDtypeStruct((3, 8, 24, 128), jnp.float32),
            jax.ShapeDtypeStruct((3, 2, 36, 128), jnp.float32),
            jax.ShapeDtypeStruct((3, 2, 36, 128), jnp.float32),
        ),
        compiler_params=pltpu.CompilerParams(vmem_limit_bytes=8 * 2**20),
        cost_estimate=pl.CostEstimate(flops=0, bytes_accessed=40 * 10**6, transcendentals=0),
    )(velocity, behind, ahead)


def advance(spacing_ref, padded_ref, behind_ref, ahead_ref, field_ref, even, odd, tend):
    even[...] = jnp.zeros(even.shape, jnp.float32)
    odd[...] = jnp.zeros(odd.shape, jnp.float32)
    even[:, 6:14, :, :] = padded_ref[...]
    for source, starts in ((behind_ref, (0, 2, 4)), (ahead_ref, (18, 16, 14))):
        even[:, starts[0] : starts[0] + 2, 6:14, :] = source[:, :, 0:8, :]
        even[:, starts[1] : starts[1] + 2, 4:16, :] = source[:, :, 8:20, :]
        even[:, starts[2] : starts[2] + 2, 2:18, :] = source[:, :, 20:36, :]
    lower, upper = spacing_ref[:, 0:128], spacing_ref[:, 1:129]
    y = lax.broadcasted_iota(jnp.int32, (1, 128), 1)
    slope = 1.0 / (lower + upper)
    slope_up = jnp.where(y < 127, slope, 0.0)
    slope_down = jnp.where(y > 0, slope, 0.0)
    curve_up = 2.0 * slope_up / upper
    curve_down = 2.0 * slope_down / lower
    curve_own = 2.0 * slope * (1.0 / upper + 1.0 / lower) + 5.0

    for section in range(3):
        source = odd if section == 1 else even
        first, count = 2 + 2 * section, 16 - 4 * section
        start, length = (2, 16) if section < 2 else (6, 8)
        span = slice(start, start + length)

        @pl.loop(first, first + count, unroll=4)
        def _(x):
            speed = [source[c, x, span, :] for c in range(3)]
            for c in range(3):
                own = speed[c]
                west, east = source[c, x - 1, span, :], source[c, x + 1, span, :]
                west_far, east_far = source[c, x - 2, span, :], source[c, x + 2, span, :]
                south = source[c, x, start - 1 : start - 1 + length, :]
                north = source[c, x, start + 1 : start + 1 + length, :]
                south_far = source[c, x, start - 2 : start - 2 + length, :]
                north_far = source[c, x, start + 2 : start + 2 + length, :]
                beneath = pltpu.roll(own, 1, 1)
                overhead = pltpu.roll(own, 127, 1)
                grad_x = (8.0 * (east - west) - (east_far - west_far)) * (1.0 / 12.0)
                grad_z = (8.0 * (north - south) - (north_far - south_far)) * (1.0 / 12.0)
                grad_y = overhead * slope_up - beneath * slope_down
                near = (east + west) + (north + south)
                far = (east_far + west_far) + (north_far + south_far)
                curve = (16.0 * near - far) * (1.0 / 12.0)
                curve = curve + overhead * curve_up + beneath * curve_down - own * curve_own
                advect = speed[0] * grad_x + speed[1] * grad_y + speed[2] * grad_z
                rate = viscosity * curve - advect
                if c == 0:
                    rate = rate + forcing
                change = gammas[section] * rate
                if section == 1:
                    change = change + zetas[1] * tend[c, x]
                if section == 2:
                    change = change + zetas[2] * tend[c, x, 4:12, :]
                result = own + step_size * change
                if section < 2:
                    tend[c, x] = rate
                    (even if section == 1 else odd)[c, x, span, :] = result
                else:
                    field_ref[pl.ds(pl.multiple_of((c * 8 + x - 6) * 8, 8), 8), :] = result


places = {(i, j): (i, j) for i in range(4) for j in range(i, 4)}
places.update({(4, 4): (1, 0), (2, 4): (2, 0), (3, 4): (2, 1), (0, 4): (3, 0), (1, 4): (3, 1)})
contract_last = (((1,), (1,)), ((), ()))
whole = pl.BlockSpec(memory_space=pltpu.VMEM)


def load_kernel(basis_ref, stored_ref, modes, snaps, sems):
    copies = []
    for chunk in range(6):
        span = pl.ds(32 * chunk, 32)
        copies += [
            pltpu.make_async_copy(basis_ref.at[:, span, :], modes.at[chunk], sems.at[0, chunk]),
            pltpu.make_async_copy(stored_ref.at[:, span, :], snaps.at[chunk], sems.at[1, chunk]),
        ]
    for copy in copies:
        copy.start()
    for copy in copies:
        copy.wait()


def loaded_parts(basis, stored):
    return pl.pallas_call(
        load_kernel,
        in_specs=[pl.BlockSpec(memory_space=pl.ANY)] * 2,
        out_specs=(whole, whole),
        out_shape=(
            jax.ShapeDtypeStruct((6, 128, 32, 128), jnp.bfloat16),
            jax.ShapeDtypeStruct((6, 40, 32, 128), jnp.bfloat16),
        ),
        scratch_shapes=[pltpu.SemaphoreType.DMA((2, 6))],
        compiler_params=pltpu.CompilerParams(vmem_limit_bytes=42 * 2**20),
        cost_estimate=pl.CostEstimate(flops=0, bytes_accessed=16 * 10**6, transcendentals=0),
    )(basis, stored)


def gram_kernel(
    picks_ref, basis_ref, stored_ref, spacing_ref, padded_ref, behind_ref, ahead_ref,
    packed_ref, turned_ref, fresh_ref, even, odd, tend,
):
    f32, bf16 = jnp.float32, jnp.bfloat16
    advance(spacing_ref, padded_ref, behind_ref, ahead_ref, fresh_ref, even, odd, tend)

    def step(chunk, total):
        for half in range(2):
            for group in range(10):
                rows = slice(16 * half, 16 * half + 16)
                place = slice(32 * chunk + 16 * half, 32 * chunk + 16 * half + 16)
                if group < 8:
                    tile = basis_ref[chunk, 16 * group : 16 * group + 16, rows, :]
                else:
                    first = 16 * (group - 8)
                    tile = jnp.stack(
                        [
                            stored_ref[chunk, picks_ref[first + j], rows, :]
                            if first + j < 31
                            else fresh_ref[place, :].astype(bf16)
                            for j in range(16)
                        ],
                        axis=0,
                    )
                tile = jnp.swapaxes(tile, 0, 1)
                for s in range(16):
                    lanes = slice(2048 * half + 128 * s, 2048 * half + 128 * s + 128)
                    turned_ref[chunk, 16 * group : 16 * group + 16, lanes] = tile[s]
            block = turned_ref[chunk, :, 2048 * half : 2048 * half + 2048]
            total = total + lax.dot_general(
                block, block, contract_last, preferred_element_type=f32
            )
        return total

    total = jnp.zeros((160, 160), f32)
    for chunk in range(6):
        total = step(chunk, total)
    lanes = lax.broadcasted_iota(jnp.int32, (32, 128), 1)
    right = jnp.concatenate([total[:, 128:160], jnp.zeros((160, 96), f32)], axis=1)
    parts = [jnp.where(lanes >= 32 * p, total[32 * p : 32 * p + 32, 0:128], 0.0) for p in range(4)]
    for p in range(5):
        r, c = places[(p, 4)]
        part = right[32 * p : 32 * p + 32, :]
        parts[r] = parts[r] + (pltpu.roll(part, 32 * c, 1) if c else part)
    for r in range(16):
        packed_ref[:, 128 * r : 128 * r + 128] = parts[r // 4][8 * (r % 4) : 8 * (r % 4) + 8, :]


def local_gram(picks, *operands):
    return pl.pallas_call(
        gram_kernel,
        in_specs=[pl.BlockSpec(memory_space=pltpu.SMEM)] + [whole] * 6,
        out_specs=(whole, whole, whole),
        out_shape=(
            jax.ShapeDtypeStruct((8, 2048), jnp.float32),
            jax.ShapeDtypeStruct((6, 160, 4096), jnp.bfloat16),
            jax.ShapeDtypeStruct((192, 128), jnp.float32),
        ),
        scratch_shapes=[
            pltpu.VMEM((3, 20, 24, 128), jnp.float32),
            pltpu.VMEM((3, 20, 24, 128), jnp.float32),
            pltpu.VMEM((3, 20, 16, 128), jnp.float32),
        ],
        compiler_params=pltpu.CompilerParams(vmem_limit_bytes=16 * 2**20),
        cost_estimate=pl.CostEstimate(flops=2 * 10**9, bytes_accessed=16 * 10**6, transcendentals=0),
    )(picks, *operands)


def factor_kernel(rows_total, sums_ref, factor_ref, left_ref, right_ref, work, side):
    f32 = jnp.float32
    lanes8 = lax.broadcasted_iota(jnp.int32, (8, 128), 1)
    subs8 = lax.broadcasted_iota(jnp.int32, (8, 128), 0)
    lanes = lax.broadcasted_iota(jnp.int32, (32, 128), 1)
    rows = lax.broadcasted_iota(jnp.int32, (32, 128), 0)
    def loaded(r):
        tiles = [
            jnp.concatenate([sums_ref[j, :, 128 * q : 128 * q + 128] for j in range(8)], axis=0)
            for q in range(4 * r, 4 * r + 4)
        ]
        return jnp.concatenate(tiles, axis=0) / rows_total

    gathered = [loaded(r) for r in range(4)]
    for p in range(4):
        work[32 * p : 32 * p + 32, :] = jnp.where(lanes >= 32 * p, gathered[p], 0.0)
        r, c = places[(p, 4)]
        last = pltpu.roll(gathered[r], 128 - 32 * c, 1) if c else gathered[r]
        side[32 * p : 32 * p + 32, :] = jnp.where(lanes < 32, last, 0.0)
    work[128:160, :] = jnp.zeros((32, 128), f32)
    last = gathered[places[(4, 4)][0]]
    side[128:160, :] = jnp.where(lanes < 32, last, 0.0)

    for p in range(5):
        base = 32 * p
        main = [work[base + 8 * g : base + 8 * g + 8, :] for g in range(4)]
        tail = [side[base + 8 * g : base + 8 * g + 8, :] for g in range(4)]
        scale = [None] * 4
        for gk in range(4):
            own, other = (main, tail) if p < 4 else (tail, main)
            first = (base if p < 4 else 0) + 8 * gk
            spread = lambda value, j: jnp.broadcast_to(value[:, j : j + 1], (8, 128))
            pick = lambda value, i: jnp.broadcast_to(value[i : i + 1, :], (8, 128))
            cols = {g: [spread(own[g], first + j) for j in range(8)] for g in range(gk, 4)}
            low = {(i, j): pick(cols[gk][j], i) for j in range(8) for i in range(j, 8)}
            own_rows = [pick(own[gk], i) for i in range(8)]
            other_rows = [pick(other[gk], i) for i in range(8)]
            inside = (lanes8 >= first) & (lanes8 < first + 8)
            solved_rows = [
                jnp.where(inside, jnp.where(lanes8 == first + i, 1.0, 0.0), own_rows[i])
                for i in range(8)
            ]
            roots = []
            for j in range(8):
                root = lax.rsqrt(low[j, j])
                inv = root * root
                roots.append(root)
                coef = {i: low[i, j] * inv for i in range(j + 1, 8)}
                for i in range(j + 1, 8):
                    for m in range(j + 1, i + 1):
                        low[i, m] = low[i, m] - coef[i] * low[m, j]
                    own_rows[i] = own_rows[i] - coef[i] * own_rows[j]
                    solved_rows[i] = solved_rows[i] - coef[i] * solved_rows[j]
                    other_rows[i] = other_rows[i] - coef[i] * other_rows[j]
                for g in range(gk + 1, 4):
                    for m in range(j + 1, 8):
                        cols[g][m] = cols[g][m] - coef[m] * cols[g][j]
                    factor_col = cols[g][j] * inv
                    if j == 0:
                        own[g] = jnp.where(inside, 0.0, own[g])
                    own[g] = own[g] - factor_col * solved_rows[j]
                    other[g] = other[g] - factor_col * other_rows[j]
            new_own, new_other, new_scale = None, None, None
            for i in range(8):
                mixed = jnp.where(inside & (lanes8 > first + i), own_rows[i], solved_rows[i])
                new_own = mixed if i == 0 else jnp.where(subs8 == i, mixed, new_own)
                new_other = other_rows[i] if i == 0 else jnp.where(subs8 == i, other_rows[i], new_other)
                new_scale = roots[i] if i == 0 else jnp.where(subs8 == i, roots[i], new_scale)
            own[gk], other[gk], scale[gk] = new_own, new_other, new_scale
        mainp = jnp.concatenate(main, axis=0)
        tailp = jnp.concatenate(tail, axis=0)
        scalep = jnp.concatenate(scale, axis=0)
        if p < 4:
            diag = lanes == rows + base
            scaled = mainp * scalep
            upper = jnp.where(lanes > rows + base, scaled, jnp.where(diag, 1.0 / scalep, 0.0))
            full_main = jnp.where((lanes > rows + base) & (lanes < base + 32), 0.0, scaled)
            side_out = tailp * scalep
            factor_ref[base : base + 32, 0:128] = upper
            factor_ref[base : base + 32, 128:160] = side_out[:, 0:32]
            both = jnp.concatenate([upper, side_out], axis=1)
            solved = jnp.concatenate([full_main, side_out], axis=1)
            block = (lanes >= base) & (lanes < base + 32)

            def reduce_rows(start, stop):
                change = lax.dot_general(
                    both[:, start:stop], solved, (((0,), (0,)), ((), ())),
                    precision=lax.Precision.HIGHEST, preferred_element_type=f32,
                )
                for q in range(start // 32, stop // 32):
                    span = slice(32 * q, 32 * q + 32)
                    part = change[32 * q - start : 32 * q - start + 32, :]
                    work[span, :] = jnp.where(block, 0.0, work[span, :]) - part[:, 0:128]
                    side[span, :] = side[span, :] - part[:, 128:256]

            reduce_rows(base + 32, base + 64)
            if p < 3:
                reduce_rows(base + 64, 160)
        else:
            diag = lanes == rows
            factor_ref[128:160, 0:128] = jnp.zeros((32, 128), f32)
            factor_ref[128:160, 128:160] = jnp.where(
                lanes > rows, tailp * scalep, jnp.where(diag, 1.0 / scalep, 0.0)
            )[:, 0:32]
            left_ref[...] = (mainp * scalep).astype(jnp.bfloat16)
            right_ref[...] = jnp.where(lanes <= rows, tailp * scalep, 0.0).astype(jnp.bfloat16)


def spread(left_ref, right_ref, turned_ref, out_ref, result, sems):
    f32, bf16 = jnp.float32, jnp.bfloat16
    coef = jnp.concatenate([left_ref[...], right_ref[:, 0:32]], axis=1)

    def copy(chunk):
        span = pl.ds(pl.multiple_of(32 * chunk, 32), 32)
        return pltpu.make_async_copy(result.at[chunk], out_ref.at[:, span, :], sems.at[chunk])

    @pl.loop(0, 6, unroll=3)
    def _(chunk):
        total = jnp.dot(coef, turned_ref[chunk], preferred_element_type=f32).astype(bf16)
        for group in range(2):
            for half in range(2):
                tile = jnp.stack(
                    [
                        total[
                            16 * group : 16 * group + 16,
                            2048 * half + 128 * s : 2048 * half + 128 * s + 128,
                        ]
                        for s in range(16)
                    ],
                    axis=0,
                )
                result[chunk, 16 * group : 16 * group + 16, 16 * half : 16 * half + 16, :] = jnp.swapaxes(tile, 0, 1)
        copy(chunk).start()

    @pl.loop(0, 6)
    def _(chunk):
        copy(chunk).wait()


def last_kernel(
    rows_total, sums_ref, turned_ref, factor_ref, out_ref, work, side, left, right, result, sems
):
    factor_kernel(rows_total, sums_ref, factor_ref, left, right, work, side)
    spread(left, right, turned_ref, out_ref, result, sems)


def finish(sums, turned, rows_total):
    return pl.pallas_call(
        functools.partial(last_kernel, rows_total),
        in_specs=[whole, whole],
        out_specs=(whole, pl.BlockSpec(memory_space=pl.ANY)),
        out_shape=(
            jax.ShapeDtypeStruct((160, 160), jnp.float32),
            jax.ShapeDtypeStruct((32, 192, 128), jnp.bfloat16),
        ),
        scratch_shapes=[
            pltpu.VMEM((160, 128), jnp.float32),
            pltpu.VMEM((160, 128), jnp.float32),
            pltpu.VMEM((32, 128), jnp.bfloat16),
            pltpu.VMEM((32, 128), jnp.bfloat16),
            pltpu.VMEM((6, 32, 32, 128), jnp.bfloat16),
            pltpu.SemaphoreType.DMA((6,)),
        ],
        compiler_params=pltpu.CompilerParams(vmem_limit_bytes=16 * 2**20),
    )(sums, turned)


def everyone(value, axis):
    count = lax.axis_size(axis)
    copies = jnp.broadcast_to(value.reshape(1, 1, -1), (count, 1, value.size))
    return lax.all_to_all(copies, axis, 0, 0)


def added(pieces):
    return functools.reduce(jnp.add, [pieces[i] for i in range(pieces.shape[0])])


def body(velocity, spacing, basis, history, picks):
    modes, stored = basis.shape[0], history.shape[0]
    rows_total = float(velocity.size * lax.axis_size("gx") * lax.axis_size("gz"))
    behind, ahead = neighbours(velocity, velocity[:, :, 0:6], "gz")
    own = jnp.pad(velocity, ((0, 0), (0, 0), (6, 10), (0, 0)))
    padded, last, first = edges(own, behind, ahead)
    behind, ahead = neighbours(last, first, "gx")
    packed, turned, field = local_gram(
        picks,
        *loaded_parts(basis.reshape(modes, -1, 128), history.reshape(stored, -1, 128)),
        spacing.reshape(1, -1),
        padded,
        behind,
        ahead,
    )
    mine = added(lax.all_to_all(packed.reshape(8, 1, -1), "gx", 0, 0))
    mine = added(everyone(mine, "gz"))
    factor, directions = finish(everyone(mine, "gx"), turned, rows_total)
    return (field.reshape(velocity.shape), factor, directions.reshape((32,) + velocity.shape))


def solution(mesh):
    return jax.shard_map(
        body,
        mesh=mesh,
        in_specs=(
            P(None, "gx", "gz", None),
            P(),
            P(None, None, "gx", "gz", None),
            P(None, None, "gx", "gz", None),
            P(),
        ),
        out_specs=(P(None, "gx", "gz", None), P(), P(None, None, "gx", "gz", None)),
        check_vma=False,
    )
```
